32 devices in a mesh: pipe: 2 (over core), seq: 4 (over z), tensor: 4 (over y, x).
Axes of the slice: x: 2, y: 2, z: 4, core: 2. Of those that a mesh axis runs over, the one named last changes fastest.
Arguments:
- frames: bfloat16 [2, 2560, 768], P(None, ('seq', 'tensor')), may hold values from -6 to 6
- clip_ids: int32 [2, 2560], P(None, 'seq'), may hold values from 0 to 2, as said below
- cotangent: bfloat16 [2, 2560, 768], P(None, ('seq', 'tensor')), may hold values from -6 to 6
- norm_gains: float32 [2, 2, 768], P('pipe'), may hold values from 0.25 to 1.75
- norm_shifts: float32 [2, 4, 768], P('pipe'), may hold values from -1.5 to 1.5
- query_projection_weight: bfloat16 [2, 768, 768], P('pipe', None, 'tensor'), may hold values from -0.4375 to 0.4375
- w_keyval: bfloat16 [2, 2, 768, 768], P('pipe', None, None, 'tensor'), may hold values from -0.21875 to 0.21875
- proj_bias: float32 [2, 2, 768], P('pipe', None, 'tensor'), may hold values from -0.3 to 0.3
- w_output: bfloat16 [2, 768, 768], P('pipe', 'tensor'), may hold values from -3 to 3
- w_expand: bfloat16 [2, 768, 3072], P('pipe', None, 'tensor'), may hold values from -0.21875 to 0.21875
- expand_bias: float32 [2, 3072], P('pipe', 'tensor'), may hold values from -2.5 to 2.5
- w_reduce: bfloat16 [2, 3072, 768], P('pipe', 'tensor'), may hold values from -0.109375 to 0.109375
Outputs:
- states: bfloat16 [2, 2, 2560, 768], P('pipe', None, ('seq', 'tensor'))
- input_grads: bfloat16 [2, 2, 2560, 768], P('pipe', None, ('seq', 'tensor'))
- grad_gains: float32 [2, 2, 768], P('pipe')
- grad_shifts: float32 [2, 4, 768], P('pipe')
- grad_query: float32 [2, 768, 768], P('pipe', None, 'tensor')
- grad_keyval: float32 [2, 2, 768, 768], P('pipe', None, None, 'tensor')
- grad_proj_bias: float32 [2, 2, 768], P('pipe', None, 'tensor')
- grad_output: float32 [2, 768, 768], P('pipe', 'tensor')
- grad_expand: float32 [2, 768, 3072], P('pipe', None, 'tensor')
- grad_expand_bias: float32 [2, 3072], P('pipe', 'tensor')
- grad_reduce: float32 [2, 3072, 768], P('pipe', 'tensor')
The draws below stay inside these ranges and needn't reach their ends.
Inputs may be any that keep to these rules, and one draw needn't show every extreme that they name: `clip_ids`: in each micro-batch the ids start at 0, never fall, and rise by one at the first frame of each clip; every clip has exactly 1500 frames except the first and the last of a micro-batch, which may have fewer; each micro-batch holds at least one whole clip; the largest id of some micro-batch is (2).
All inputs are finite; a program needn't handle non-finite values.
Results may differ from the reference program's by a relative error of at most 0.035.
Values may be sent and summed in bfloat16 or wider, within the bound.
A program may use at most 128 MiB of HBM per device.

```python
import math
import jax
import jax.numpy as jnp
from jax import lax

D = 768
HEAD_DIM = 64
FF = 3072
TOK_DEV = 640
MICRO = 2
CLIP = 1500
REACH = 3
FRAMES = 2560


def draw_clip_ids(key, part):
    key = jax.random.fold_in(key, 7)
    block_key, inner_key, early_key = jax.random.split(key, 3)
    block_pick = jax.random.randint(block_key, (MICRO, 1), 0, (FRAMES - CLIP) // TOK_DEV)
    inner_pick = jax.random.randint(inner_key, (MICRO, 1), REACH * TOK_DEV - CLIP + 1, TOK_DEV)
    later_start = block_pick * TOK_DEV + inner_pick
    early_top = max((FRAMES - 1) % CLIP, 1)
    early_start = jax.random.randint(early_key, (MICRO, 1), 1, early_top + 1)
    row_index = jnp.arange(MICRO, dtype=jnp.int32)[:, None]
    whole_start = jnp.where(row_index == 0, early_start, later_start).astype(jnp.int32)
    margin = (FRAMES // CLIP + 2) * CLIP
    position = jnp.arange(FRAMES, dtype=jnp.int32)[None, :]
    return ((position - whole_start + margin) // CLIP - (margin - whole_start) // CLIP).astype(jnp.int32)


def block_levels(stream_key, extent, shards, least, top_value):
    factor_of, own = 1.0, jax.random.fold_in(stream_key, 6)
    for dim, blocks in shards:
        draws = jnp.exp(jax.random.uniform(jax.random.fold_in(own, dim), (blocks,), jnp.float32, least / len(shards), top_value / len(shards)))
        factor_of = factor_of * jnp.repeat(draws, extent[dim] // blocks).reshape([-1 if axis == dim else 1 for axis in range(len(extent))])
    return factor_of


def gaussian(key, shape, width, most, shards=(), held_as=jnp.bfloat16):
    values = jax.random.normal(key, shape, jnp.float32) * width
    if len(shards) > 0:
        values = block_levels(key, shape, shards, -0.22, 0.18) * values
    return jnp.clip(values, min=-most, max=most).astype(held_as)


def setup_inputs(seed: int = 0) -> dict:
    arg_keys = jax.random.split(jax.random.key(seed), 13)
    frames = gaussian(arg_keys[0], (MICRO, FRAMES, D), 1.0, 6.0, ((1, 16),))
    clip_ids = draw_clip_ids(jax.random.fold_in(arg_keys[12], 71), 0)
    cotangent = gaussian(arg_keys[2], (MICRO, FRAMES, D), 1.0, 6.0, ((1, 16),))
    norm_gains = jnp.clip(1.0 + 0.15 * jax.random.normal(arg_keys[3], (2, 2, D), jnp.float32), 0.25, 1.75)
    norm_shifts = gaussian(arg_keys[4], (2, 4, D), 0.3, 1.5, ((0, 2),), jnp.float32)
    query_projection_weight = gaussian(arg_keys[5], (2, D, D), (D // 4) ** -0.5, 0.4375, ((0, 2), (2, 4)))
    w_keyval = gaussian(arg_keys[6], (2, 2, D, D), D ** -0.5, 0.21875, ((0, 2), (3, 4)))
    proj_bias = gaussian(arg_keys[7], (2, 2, D), 0.05, 0.3, ((0, 2), (2, 4)), jnp.float32)
    w_output = gaussian(arg_keys[8], (2, D, D), 4 ** -0.5, 3.0, ((0, 2), (1, 4)))
    w_expand = gaussian(arg_keys[9], (2, D, FF), D ** -0.5, 0.21875, ((0, 2), (2, 4)))
    expand_bias = gaussian(arg_keys[10], (2, FF), 0.5, 2.5, ((0, 2), (1, 4)), jnp.float32)
    w_reduce = gaussian(arg_keys[11], (2, FF, D), FF ** -0.5, 0.109375, ((0, 2), (1, 4)))
    return dict(frames=frames, clip_ids=clip_ids, cotangent=cotangent, norm_gains=norm_gains, norm_shifts=norm_shifts, query_projection_weight=query_projection_weight, w_keyval=w_keyval, proj_bias=proj_bias, w_output=w_output, w_expand=w_expand, expand_bias=expand_bias, w_reduce=w_reduce)


EPS = 1e-05
NEG = -1e+30
HIGH = lax.Precision.HIGHEST

@jax.custom_vjp
def low(v):
    return lax.optimization_barrier(v.astype(jnp.bfloat16)).astype(jnp.float32)

@jax.custom_vjp
def low_back(v):
    return v

def low_keep(v):
    return (low(v), None)

def low_pass(kept, grad):
    return (grad,)

def back_keep(v):
    return (v, None)

def back_low(kept, grad):
    return (low(grad),)
low.defvjp(low_keep, low_pass)
low_back.defvjp(back_keep, back_low)

def matmul(left, right):
    return jnp.dot(left, right, preferred_element_type=jnp.float32, precision=HIGH)

def layer_norm(values_in, gain, shift):
    center = values_in - lax.optimization_barrier(jnp.mean(values_in, axis=-1, keepdims=True))
    spread = lax.optimization_barrier(jnp.mean(center * center, axis=-1, keepdims=True))
    return center * lax.rsqrt(spread + EPS) * gain + shift

def attend(query, keys_here, values_here, clip_row):
    frame_count = query.shape[0]
    head_count = query.shape[1] // HEAD_DIM
    block_rows = math.gcd(frame_count, 512)
    factor = HEAD_DIM ** (-0.5)
    query_blocks = query.reshape(frame_count // block_rows, block_rows, head_count, HEAD_DIM)
    clip_blocks = clip_row.reshape(frame_count // block_rows, block_rows)
    key_heads = keys_here.reshape(frame_count, head_count, HEAD_DIM)
    value_heads = values_here.reshape(frame_count, head_count, HEAD_DIM)

    def one_block(items):
        query_blk, clip_blk = items
        scores = low_back(jnp.einsum('qhd,khd->hqk', query_blk, key_heads, precision=HIGH) * factor)
        same_clip = (clip_blk[:, None] == clip_row[None, :])[None]
        scores = jnp.where(same_clip, scores, NEG)
        row_top = lax.optimization_barrier(jnp.max(scores, axis=-1, keepdims=True))
        expos = jnp.exp(scores - row_top)
        probs = low(expos / lax.optimization_barrier(jnp.sum(expos, axis=-1, keepdims=True)))
        return jnp.einsum('hqk,khd->qhd', probs, value_heads, precision=HIGH)
    result = lax.map(jax.checkpoint(one_block), (query_blocks, clip_blocks))
    return result.reshape(frame_count, head_count * HEAD_DIM)

def layer(resid_in, gains, shifts, query_weight, keyval_w, bias_pair, output_w, expand_w, expand_b, reduce_w, clip_row):
    normed = low(layer_norm(resid_in, gains[0], shifts[0]))
    query = low(low_back(matmul(normed, query_weight) + bias_pair[0]))
    keys_here = low(low_back(matmul(normed, keyval_w[0])))
    values_here = low(low_back(matmul(normed, keyval_w[1]) + bias_pair[1]))
    mixed = low(low_back(attend(query, keys_here, values_here, clip_row)))
    resid_mid = resid_in + low_back(matmul(mixed, output_w)) + shifts[2]
    normed_mid = low(layer_norm(resid_mid, gains[1], shifts[1]))
    expanded = low_back(matmul(normed_mid, expand_w) + expand_b)
    activated = low(jax.nn.gelu(expanded, approximate=False))
    return resid_mid + matmul(activated, reduce_w) + shifts[3]

def reference(frames, clip_ids, cotangent, norm_gains, norm_shifts, query_projection_weight, w_keyval, proj_bias, w_output, w_expand, expand_bias, w_reduce):
    params = tuple((member.astype(jnp.float32) for member in (norm_gains, norm_shifts, query_projection_weight, w_keyval, proj_bias, w_output, w_expand, expand_bias, w_reduce)))
    frames_wide = frames.astype(jnp.float32)
    cot_wide = cotangent.astype(jnp.float32)
    probe = jnp.zeros_like(frames_wide)

    def forward(frames_in, probe_in, *weights):
        firsts = []
        seconds = []
        for number in range(MICRO):
            first_out = low(layer(frames_in[number], *[member[0] for member in weights], clip_ids[number]))
            first_out = low_back(first_out + probe_in[number])
            firsts.append(first_out)
            seconds.append(layer(first_out, *[member[1] for member in weights], clip_ids[number]))
        return (jnp.stack(seconds), jnp.stack(firsts))
    (second, first), pullback = jax.vjp(forward, frames_wide, probe, *params)
    gradients = pullback((cot_wide, jnp.zeros_like(first)))
    states = jnp.stack([first, second]).astype(jnp.bfloat16)
    input_grads = jnp.stack([gradients[0], gradients[1]]).astype(jnp.bfloat16)
    return (states, input_grads, gradients[2], gradients[3], gradients[4], gradients[5], gradients[6], gradients[7], gradients[8], gradients[9], gradients[10])
```

```python
import jax
import jax.numpy as jnp
from jax import lax
from jax.experimental import pallas as pl
from jax.experimental.pallas import tpu as pltpu
from jax.sharding import PartitionSpec as P

HEAD_DIM = 64
REACH = 3
KEY_TILE = 128


EPS = 1e-05
NEG = -1e30


def norm_rows(values_in, gain, shift):
    center = values_in - jnp.mean(values_in, axis=-1, keepdims=True)
    spread = jnp.mean(center * center, axis=-1, keepdims=True)
    return center * lax.rsqrt(spread + EPS) * gain + shift


def gelu_exact(values_in):
    return jax.nn.gelu(values_in, approximate=False)


def matmul(left, right):
    return jnp.dot(left, right, preferred_element_type=jnp.float32)


def inner_rows(left, right):
    return lax.dot_general(
        left, right, (((0,), (0,)), ((), ())), preferred_element_type=jnp.float32
    )


def times_trans(left, right):
    return lax.dot_general(
        left, right, (((1,), (1,)), ((), ())), preferred_element_type=jnp.float32
    )


def spread_rows(piece):
    return lax.all_gather(piece, "tensor", axis=0, tiled=True)


def fold_rows(partial_sum):
    return lax.psum_scatter(
        partial_sum.astype(jnp.bfloat16), "tensor", scatter_dimension=0, tiled=True
    ).astype(jnp.float32)


def swap_cores(block):
    return lax.ppermute(block, "pipe", [(0, 1), (1, 0)])


def shifted(block, distance):
    devices = range(lax.axis_size("seq"))
    route = [(i - distance, i) for i in devices if i - distance in devices]
    return lax.ppermute(block, "seq", route)


def whole_row():
    return lax.axis_size("seq") <= 2 * REACH + 1


def gather_window(block):
    if whole_row():
        return lax.all_gather(block, "seq", axis=0, tiled=True)
    return jnp.concatenate(
        [block if o == 0 else shifted(block, o) for o in range(REACH, -REACH - 1, -1)], axis=0
    )


def return_window(terms):
    if whole_row():
        return lax.psum_scatter(terms, "seq", scatter_dimension=0, tiled=True)
    pieces = jnp.split(terms, 2 * REACH + 1, axis=0)
    total = 0.0
    for piece, offset in zip(pieces, range(REACH, -REACH - 1, -1)):
        got = piece if offset == 0 else shifted(piece, -offset)
        total = total + got.astype(jnp.float32)
    return total.astype(jnp.bfloat16)


def head_parts(matrix, axis):
    head = lax.broadcasted_iota(jnp.int32, matrix.shape, axis) // HEAD_DIM
    return [
        jnp.where(head == h, matrix, 0.0).astype(jnp.bfloat16)
        for h in range(matrix.shape[axis] // HEAD_DIM)
    ]


def attend_kernel(span, keys, values_t, query_t, key_marks, marks, mixed_t, logs, held):
    rows = query_t.shape[1]
    parts = head_parts(query_t[...].astype(jnp.float32) * HEAD_DIM**-0.5, 0)
    held[...] = jnp.zeros_like(held)
    logs[...] = jnp.zeros_like(logs)

    def step(number, carry):
        start = pl.multiple_of(number * KEY_TILE, KEY_TILE)
        key = keys[pl.ds(start, KEY_TILE), :]
        value = values_t[:, pl.ds(start, KEY_TILE)]
        same = key_marks[pl.ds(start, KEY_TILE), :] == marks[...]
        later = []
        for h, part in enumerate(parts):
            top, total = carry[h]
            scores = jnp.where(same, matmul(key, part), NEG)
            new_top = jnp.maximum(top, jnp.max(scores, axis=0, keepdims=True))
            weights = jnp.exp(scores - new_top)
            scale = jnp.exp(top - new_top)
            total = total * scale + jnp.sum(weights, axis=0, keepdims=True)
            own = pl.ds(h * HEAD_DIM, HEAD_DIM)
            held[own, :] = held[own, :] * scale + matmul(
                value[h * HEAD_DIM : (h + 1) * HEAD_DIM, :], weights.astype(jnp.bfloat16)
            )
            later.append((new_top, total))
        return tuple(later)

    first = tuple(
        (jnp.full((1, rows), NEG, jnp.float32), jnp.zeros((1, rows), jnp.float32)) for _ in parts
    )
    last = lax.fori_loop(span[0], span[1], step, first)
    for h, (top, total) in enumerate(last):
        own = pl.ds(h * HEAD_DIM, HEAD_DIM)
        mixed_t[own, :] = (held[own, :] / total).astype(jnp.bfloat16)
        logs[pl.ds(h, 1), :] = top + jnp.log(total)


def attend_back_kernel(
    span, keys, keys_t, values, query, query_t, grad, grad_t, mixed_t, logs, key_marks, marks,
    query_grad_t, key_grad, value_grad, held,
):
    factor = HEAD_DIM**-0.5
    query_parts = head_parts(query[...].astype(jnp.float32) * factor, 1)
    query_t_parts = head_parts(query_t[...].astype(jnp.float32) * factor, 0)
    grad_parts = head_parts(grad[...].astype(jnp.float32), 1)
    grad_t_parts = head_parts(grad_t[...].astype(jnp.float32), 0)
    product = grad_t[...].astype(jnp.float32) * mixed_t[...].astype(jnp.float32)
    deltas = [
        jnp.sum(product[h * HEAD_DIM : (h + 1) * HEAD_DIM, :], axis=0, keepdims=True)
        for h in range(len(query_parts))
    ]
    held[...] = jnp.zeros_like(held)
    key_grad[...] = jnp.zeros_like(key_grad)
    value_grad[...] = jnp.zeros_like(value_grad)

    def step(number, carry):
        start = pl.multiple_of(number * KEY_TILE, KEY_TILE)
        here = pl.ds(start, KEY_TILE)
        key = keys[here, :]
        key_t = keys_t[:, here]
        value = values[here, :]
        same = key_marks[here, :] == marks[...]
        key_total = jnp.zeros(key.shape, jnp.float32)
        value_total = jnp.zeros(key.shape, jnp.float32)
        for h in range(len(query_parts)):
            scores = matmul(key, query_t_parts[h])
            probs = jnp.where(same, jnp.exp(scores - logs[pl.ds(h, 1), :]), 0.0)
            grad_probs = matmul(value, grad_t_parts[h])
            grad_scores = (probs * (grad_probs - deltas[h])).astype(jnp.bfloat16)
            value_total += matmul(probs.astype(jnp.bfloat16), grad_parts[h])
            key_total += matmul(grad_scores, query_parts[h])
            own = pl.ds(h * HEAD_DIM, HEAD_DIM)
            held[own, :] += matmul(key_t[h * HEAD_DIM : (h + 1) * HEAD_DIM, :], grad_scores)
        key_grad[here, :] = key_total.astype(jnp.bfloat16)
        value_grad[here, :] = value_total.astype(jnp.bfloat16)
        return carry

    lax.fori_loop(span[0], span[1], step, 0)
    query_grad_t[...] = (held[...] * factor).astype(jnp.bfloat16)


def vmem(count):
    return [pl.BlockSpec(memory_space=pltpu.SMEM)] + [
        pl.BlockSpec(memory_space=pltpu.VMEM) for _ in range(count)
    ]


def forward_attention(query_t, keys, values_t, clips):
    span, key_marks, marks = clips
    width, rows = query_t.shape
    return pl.pallas_call(
        attend_kernel,
        out_shape=(
            jax.ShapeDtypeStruct((width, rows), jnp.bfloat16),
            jax.ShapeDtypeStruct((8, rows), jnp.float32),
        ),
        in_specs=vmem(5),
        out_specs=tuple(vmem(2)[1:]),
        scratch_shapes=[pltpu.VMEM((width, rows), jnp.float32)],
        compiler_params=pltpu.CompilerParams(vmem_limit_bytes=40 * 2**20),
        name="attend",
    )(span, keys, values_t, query_t, key_marks, marks)


def backward_attention(keys, keys_t, values, query, query_t, grad, grad_t, mixed_t, logs, clips):
    span, key_marks, marks = clips
    width, rows = query_t.shape
    return pl.pallas_call(
        attend_back_kernel,
        out_shape=(
            jax.ShapeDtypeStruct((width, rows), jnp.bfloat16),
            jax.ShapeDtypeStruct(keys.shape, jnp.bfloat16),
            jax.ShapeDtypeStruct(keys.shape, jnp.bfloat16),
        ),
        in_specs=vmem(11),
        out_specs=tuple(vmem(3)[1:]),
        scratch_shapes=[pltpu.VMEM((width, rows), jnp.float32)],
        compiler_params=pltpu.CompilerParams(vmem_limit_bytes=40 * 2**20),
        name="attend_back",
    )(span, keys, keys_t, values, query, query_t, grad, grad_t, mixed_t, logs, key_marks, marks)


def clip_window(clip_here):
    marks = clip_here + 1
    key_marks = gather_window(marks)
    tiles = key_marks.reshape(-1, KEY_TILE)
    hit = jnp.any((tiles >= marks[0]) & (tiles <= marks[-1]), axis=1)
    place = jnp.arange(tiles.shape[0], dtype=jnp.int32)
    low = jnp.min(jnp.where(hit, place, tiles.shape[0]))
    high = jnp.max(jnp.where(hit, place + 1, 0))
    return (jnp.stack([low, high]), key_marks[:, None], marks[None, :])


def layer_forward(layer_in, clips, weights):
    gains, shifts, qkv_w, bias_pair, output_w, expand_w, expand_b, reduce_w = weights
    width = bias_pair.shape[-1]
    resid_in = layer_in.astype(jnp.float32)
    normed = spread_rows(norm_rows(resid_in, gains[0], shifts[0]).astype(jnp.bfloat16))
    no_bias = jnp.zeros((width,), jnp.float32)
    qkv_bias = jnp.concatenate([bias_pair[0], no_bias, bias_pair[1]])
    qkv = (matmul(normed, qkv_w) + qkv_bias).astype(jnp.bfloat16)
    query = qkv[:, :width]
    window = gather_window(qkv[:, width:])
    keys, values = window[:, :width], window[:, width:]
    query_t = query.T
    mixed_t, logs = forward_attention(query_t, keys, values.T, clips)
    resid_mid = resid_in + fold_rows(inner_rows(mixed_t, output_w)) + shifts[2]
    normed_mid = spread_rows(norm_rows(resid_mid, gains[1], shifts[1]).astype(jnp.bfloat16))
    expanded = matmul(normed_mid, expand_w) + expand_b
    activated = gelu_exact(expanded).astype(jnp.bfloat16)
    layer_out = (resid_mid + fold_rows(matmul(activated, reduce_w)) + shifts[3]).astype(
        jnp.bfloat16
    )
    saved = (
        layer_in, normed, query, query_t, keys, values, mixed_t, logs, resid_mid, normed_mid,
        expanded, activated,
    )
    return (layer_out, saved)


def layer_backward(layer_grad, saved, clips, weights):
    gains, shifts, qkv_w, bias_pair, output_w, expand_w, expand_b, reduce_w = weights
    (
        layer_in, normed, query, query_t, keys, values, mixed_t, logs, resid_mid, normed_mid,
        expanded, activated,
    ) = saved
    grad_out = layer_grad.astype(jnp.float32)
    grad_all = spread_rows(layer_grad)
    grad_act = times_trans(grad_all, reduce_w)
    gelu_back = jax.vjp(gelu_exact, expanded)[1]
    grad_expanded = gelu_back(grad_act)[0].astype(jnp.bfloat16)
    grad_normed_mid = fold_rows(times_trans(grad_expanded, expand_w))
    grad_reduce = inner_rows(activated, grad_all).astype(jnp.bfloat16)
    grad_expand_bias = jnp.sum(grad_expanded, axis=0, dtype=jnp.float32)
    grad_expand = inner_rows(normed_mid, grad_expanded).astype(jnp.bfloat16)
    feed_sum = sum_half(grad_expand, grad_reduce)
    mid_back = jax.vjp(norm_rows, resid_mid, gains[1], shifts[1])[1]
    grad_mid_norm, grad_gain_mid, grad_shift_mid = mid_back(grad_normed_mid)
    grad_mid = grad_out + grad_mid_norm
    grad_branch = spread_rows(grad_mid.astype(jnp.bfloat16))
    grad_mixed = times_trans(grad_branch, output_w).astype(jnp.bfloat16)
    query_grad_t, key_terms, value_terms = backward_attention(
        keys, keys.T, values, query, query_t, grad_mixed, grad_mixed.T, mixed_t, logs, clips
    )
    grad_output = matmul(mixed_t, grad_branch).astype(jnp.bfloat16)
    grad_keyval = return_window(jnp.concatenate([key_terms, value_terms], axis=1))
    grad_qkv = jnp.concatenate([query_grad_t.T, grad_keyval], axis=1)
    grad_normed = fold_rows(times_trans(grad_qkv, qkv_w))
    grad_qkv_w = inner_rows(normed, grad_qkv).astype(jnp.bfloat16)
    half = grad_qkv_w.shape[0] // 2
    half_out = grad_output.shape[0] // 2
    qkv_sum = sum_half(grad_qkv_w[:half], grad_qkv_w[half:])
    output_sum = sum_half(grad_output[:half_out], grad_output[half_out:])
    qkv_bias = jnp.sum(grad_qkv, axis=0, dtype=jnp.float32)
    in_back = jax.vjp(norm_rows, layer_in.astype(jnp.float32), gains[0], shifts[0])[1]
    grad_in_norm, grad_gain_in, grad_shift_in = in_back(grad_normed)
    input_grad = (grad_mid + grad_in_norm).astype(jnp.bfloat16)
    norms = jnp.stack(
        [
            grad_gain_in, grad_gain_mid, grad_shift_in, grad_shift_mid,
            jnp.sum(grad_mid, axis=0), jnp.sum(grad_out, axis=0),
        ]
    )
    biases = jnp.concatenate([qkv_bias, grad_expand_bias])
    return (input_grad, (feed_sum, qkv_sum, output_sum), norms, biases)


def sum_half(first, second):
    core = lax.axis_index("pipe") == 0
    kept = jnp.where(core, first, second)
    got = swap_cores(jnp.where(core, second, first))
    return lax.psum(kept + got, "seq")


def shards(
    frames,
    clip_ids,
    cotangent,
    norm_gains,
    norm_shifts,
    query_projection_weight,
    w_keyval,
    proj_bias,
    w_output,
    w_expand,
    expand_bias,
    w_reduce,
):
    core = lax.axis_index("pipe")
    low_core = core == 0
    qkv_w = jnp.concatenate([query_projection_weight[0], w_keyval[0, 0], w_keyval[0, 1]], axis=1)
    own = (
        norm_gains[0], norm_shifts[0], qkv_w, proj_bias[0], w_output[0], w_expand[0],
        expand_bias[0], w_reduce[0],
    )
    other = tuple(swap_cores(item) for item in own)
    weights = [
        tuple(jnp.where(low_core, a, b) for a, b in zip(own, other)),
        tuple(jnp.where(low_core, b, a) for a, b in zip(own, other)),
    ]
    clips = clip_window(lax.dynamic_index_in_dim(clip_ids, core, 0, keepdims=False))
    stream = lax.dynamic_index_in_dim(frames, core, 0, keepdims=False)
    outs, saved = [], []
    for number in range(2):
        stream, kept = layer_forward(stream, clips, weights[number])
        outs.append(stream)
        saved.append(kept)
    grad = lax.dynamic_index_in_dim(cotangent, core, 0, keepdims=False)
    grads, sums, norms, biases = [None] * 2, [None] * 2, [None] * 2, [None] * 2
    for number in (1, 0):
        grad, sums[number], norms[number], biases[number] = layer_backward(
            grad, saved[number], clips, weights[number]
        )
        grads[number] = grad

    def both_batches(pair):
        mine = jnp.where(low_core, pair[0], pair[1])
        got = swap_cores(jnp.where(low_core, pair[1], pair[0]))
        return jnp.stack([jnp.where(low_core, mine, got), jnp.where(low_core, got, mine)])[None]

    def both_halves(place):
        mine = jnp.where(low_core, sums[0][place], sums[1][place])
        got = swap_cores(jnp.where(low_core, sums[1][place], sums[0][place]))
        return (
            jnp.where(low_core, mine, got).astype(jnp.float32),
            jnp.where(low_core, got, mine).astype(jnp.float32),
        )

    states = both_batches(outs)
    input_grads = both_batches(grads)
    grad_expand, grad_reduce = both_halves(0)
    grad_qkv = jnp.concatenate(both_halves(1), axis=0)
    grad_output = jnp.concatenate(both_halves(2), axis=0)
    norm_sum = lax.psum(jnp.stack(norms), ("pipe", "seq", "tensor"))
    norm_sum = lax.dynamic_index_in_dim(norm_sum, core, 0, keepdims=False)
    bias_sum = lax.psum(jnp.stack(biases), ("pipe", "seq"))
    bias_sum = lax.dynamic_index_in_dim(bias_sum, core, 0, keepdims=False)
    width = proj_bias.shape[-1]
    return (
        states,
        input_grads,
        norm_sum[None, :2],
        norm_sum[None, 2:],
        grad_qkv[None, :, :width],
        jnp.stack([grad_qkv[:, width : 2 * width], grad_qkv[:, 2 * width :]])[None],
        jnp.stack([bias_sum[:width], bias_sum[2 * width : 3 * width]])[None],
        grad_output[None],
        grad_expand[None],
        bias_sum[None, 3 * width :],
        grad_reduce[None],
    )


def solution(mesh):
    return jax.shard_map(
        shards,
        mesh=mesh,
        in_specs=(
            P(None, ("seq", "tensor"), None),
            P(None, "seq"),
            P(None, ("seq", "tensor"), None),
            P("pipe", None, None),
            P("pipe", None, None),
            P("pipe", None, "tensor"),
            P("pipe", None, None, "tensor"),
            P("pipe", None, "tensor"),
            P("pipe", "tensor", None),
            P("pipe", None, "tensor"),
            P("pipe", "tensor"),
            P("pipe", "tensor", None),
        ),
        out_specs=(
            P("pipe", None, ("seq", "tensor"), None),
            P("pipe", None, ("seq", "tensor"), None),
            P("pipe", None, None),
            P("pipe", None, None),
            P("pipe", None, "tensor"),
            P("pipe", None, None, "tensor"),
            P("pipe", None, "tensor"),
            P("pipe", "tensor", None),
            P("pipe", None, "tensor"),
            P("pipe", "tensor"),
            P("pipe", "tensor", None),
        ),
        check_vma=False,
    )
```

```python
import functools

import jax
import jax.numpy as jnp
from jax import lax
from jax.experimental import pallas as pl
from jax.experimental.pallas import tpu as pltpu
from jax.sharding import PartitionSpec as P

HEAD_DIM = 64
REACH = 3
KEY_TILE = 128


EPS = 1e-05
NEG = -1e30


def norm_rows(values_in, gain, shift):
    center = values_in - jnp.mean(values_in, axis=-1, keepdims=True)
    spread = jnp.mean(center * center, axis=-1, keepdims=True)
    return center * lax.rsqrt(spread + EPS) * gain + shift


def gelu_exact(values_in):
    return jax.nn.gelu(values_in, approximate=False)


def matmul(left, right):
    return jnp.dot(left, right, preferred_element_type=jnp.float32)


def inner_rows(left, right):
    return lax.dot_general(
        left, right, (((0,), (0,)), ((), ())), preferred_element_type=jnp.float32
    )


def times_trans(left, right):
    return lax.dot_general(
        left, right, (((1,), (1,)), ((), ())), preferred_element_type=jnp.float32
    )


def meet(axis):
    count = lax.axis_size(axis)
    me = lax.axis_index(axis)
    peers = [lax.rem(me + step, count) for step in range(1, count)]
    barrier = pltpu.get_barrier_semaphore()
    for peer in peers:
        pl.semaphore_signal(
            barrier, inc=1, device_id={axis: peer}, device_id_type=pl.DeviceIdType.MESH
        )
    pl.semaphore_wait(barrier, count - 1)
    return (me, peers)


def push(source, target, sent, landed, axis, peer):
    copy = pltpu.make_async_remote_copy(
        src_ref=source,
        dst_ref=target,
        send_sem=sent,
        recv_sem=landed,
        device_id={axis: peer},
        device_id_type=pl.DeviceIdType.MESH,
    )
    copy.start()
    return copy


def spread_kernel(piece, whole, sent, landed):
    me, peers = meet("tensor")
    rows = piece.shape[0]
    own = pl.ds(pl.multiple_of(me * rows, rows), rows)
    copies = [
        push(piece, whole.at[own], sent.at[k], landed.at[k], "tensor", peer)
        for k, peer in enumerate(peers)
    ]
    whole[own, :] = piece[...]
    for copy in copies:
        copy.wait()


def fold_kernel(partial, total, slots, sent, landed):
    me, peers = meet("tensor")
    rows = total.shape[0]
    copies = []
    for k, peer in enumerate(peers):
        block = partial.at[pl.ds(pl.multiple_of(peer * rows, rows), rows)]
        copies.append(push(block, slots.at[k], sent.at[k], landed.at[k], "tensor", peer))
    own = pl.ds(pl.multiple_of(me * rows, rows), rows)
    total[...] = partial[own, :].astype(jnp.float32)
    for k, copy in enumerate(copies):
        copy.wait()
        total[...] += slots[k].astype(jnp.float32)


def total_kernel(axis, piece, total, slots, sent, landed):
    me, peers = meet(axis)
    copies = [
        push(piece, slots.at[me], sent.at[k], landed.at[k], axis, peer)
        for k, peer in enumerate(peers)
    ]
    slots[pl.ds(me, 1)] = piece[...][None]
    for copy in copies:
        copy.wait()
    result = slots[0]
    for k in range(1, slots.shape[0]):
        result = result + slots[k]
    total[...] = result


def exchange(kernel, item, out, slots, axis, number, name):
    count = lax.axis_size(axis)
    scratch = [] if slots is None else [pltpu.VMEM(slots, item.dtype)]
    return pl.pallas_call(
        kernel,
        out_shape=jax.ShapeDtypeStruct(*out),
        in_specs=[pl.BlockSpec(memory_space=pltpu.VMEM)],
        out_specs=pl.BlockSpec(memory_space=pltpu.VMEM),
        scratch_shapes=scratch
        + [pltpu.SemaphoreType.DMA((count - 1,)), pltpu.SemaphoreType.DMA((count - 1,))],
        compiler_params=pltpu.CompilerParams(
            collective_id=number, has_side_effects=True, vmem_limit_bytes=24 * 2**20
        ),
        name=name,
    )(item)


def spread_rows(piece):
    rows, width = piece.shape
    whole = (rows * lax.axis_size("tensor"), width)
    return exchange(spread_kernel, piece, (whole, piece.dtype), None, "tensor", 1, "spread")


def fold_rows(partial_sum):
    count = lax.axis_size("tensor")
    rows, width = partial_sum.shape[0] // count, partial_sum.shape[1]
    return exchange(
        fold_kernel, partial_sum.astype(jnp.bfloat16), ((rows, width), jnp.float32),
        (count - 1, rows, width), "tensor", 2, "fold",
    )


def total_over(item, axis, number):
    return exchange(
        functools.partial(total_kernel, axis), item, (item.shape, item.dtype),
        (lax.axis_size(axis), *item.shape), axis, number, "total_" + axis,
    )


def swap_cores(block):
    return lax.ppermute(block, "pipe", [(0, 1), (1, 0)])


def shifted(block, distance):
    devices = range(lax.axis_size("seq"))
    route = [(i - distance, i) for i in devices if i - distance in devices]
    return lax.ppermute(block, "seq", route)


def whole_row():
    return lax.axis_size("seq") <= 2 * REACH + 1


def gather_window(block):
    if whole_row():
        return lax.all_gather(block, "seq", axis=0, tiled=True)
    return jnp.concatenate(
        [block if o == 0 else shifted(block, o) for o in range(REACH, -REACH - 1, -1)], axis=0
    )


def return_window(terms):
    if whole_row():
        return lax.psum_scatter(terms, "seq", scatter_dimension=0, tiled=True)
    pieces = jnp.split(terms, 2 * REACH + 1, axis=0)
    total = 0.0
    for piece, offset in zip(pieces, range(REACH, -REACH - 1, -1)):
        got = piece if offset == 0 else shifted(piece, -offset)
        total = total + got.astype(jnp.float32)
    return total.astype(jnp.bfloat16)


def head_parts(matrix, axis):
    head = lax.broadcasted_iota(jnp.int32, matrix.shape, axis) // HEAD_DIM
    return [
        jnp.where(head == h, matrix, 0.0).astype(jnp.bfloat16)
        for h in range(matrix.shape[axis] // HEAD_DIM)
    ]


def attend_kernel(span, keys, values_t, query_t, key_marks, marks, mixed_t, logs, held):
    rows = query_t.shape[1]
    parts = head_parts(query_t[...].astype(jnp.float32) * HEAD_DIM**-0.5, 0)
    held[...] = jnp.zeros_like(held)
    logs[...] = jnp.zeros_like(logs)

    def step(number, carry):
        start = pl.multiple_of(number * KEY_TILE, KEY_TILE)
        key = keys[pl.ds(start, KEY_TILE), :]
        value = values_t[:, pl.ds(start, KEY_TILE)]
        same = key_marks[pl.ds(start, KEY_TILE), :] == marks[...]
        later = []
        for h, part in enumerate(parts):
            top, total = carry[h]
            scores = jnp.where(same, matmul(key, part), NEG)
            new_top = jnp.maximum(top, jnp.max(scores, axis=0, keepdims=True))
            weights = jnp.exp(scores - new_top)
            scale = jnp.exp(top - new_top)
            total = total * scale + jnp.sum(weights, axis=0, keepdims=True)
            own = pl.ds(h * HEAD_DIM, HEAD_DIM)
            held[own, :] = held[own, :] * scale + matmul(
                value[h * HEAD_DIM : (h + 1) * HEAD_DIM, :], weights.astype(jnp.bfloat16)
            )
            later.append((new_top, total))
        return tuple(later)

    first = tuple(
        (jnp.full((1, rows), NEG, jnp.float32), jnp.zeros((1, rows), jnp.float32)) for _ in parts
    )
    last = lax.fori_loop(span[0], span[1], step, first)
    for h, (top, total) in enumerate(last):
        own = pl.ds(h * HEAD_DIM, HEAD_DIM)
        mixed_t[own, :] = (held[own, :] / total).astype(jnp.bfloat16)
        logs[pl.ds(h, 1), :] = top + jnp.log(total)


def attend_back_kernel(
    span, keys, keys_t, values, query, query_t, grad, grad_t, mixed_t, logs, key_marks, marks,
    query_grad_t, key_grad, value_grad, held,
):
    factor = HEAD_DIM**-0.5
    query_parts = head_parts(query[...].astype(jnp.float32) * factor, 1)
    query_t_parts = head_parts(query_t[...].astype(jnp.float32) * factor, 0)
    grad_parts = head_parts(grad[...].astype(jnp.float32), 1)
    grad_t_parts = head_parts(grad_t[...].astype(jnp.float32), 0)
    product = grad_t[...].astype(jnp.float32) * mixed_t[...].astype(jnp.float32)
    deltas = [
        jnp.sum(product[h * HEAD_DIM : (h + 1) * HEAD_DIM, :], axis=0, keepdims=True)
        for h in range(len(query_parts))
    ]
    held[...] = jnp.zeros_like(held)
    key_grad[...] = jnp.zeros_like(key_grad)
    value_grad[...] = jnp.zeros_like(value_grad)

    def step(number, carry):
        start = pl.multiple_of(number * KEY_TILE, KEY_TILE)
        here = pl.ds(start, KEY_TILE)
        key = keys[here, :]
        key_t = keys_t[:, here]
        value = values[here, :]
        same = key_marks[here, :] == marks[...]
        key_total = jnp.zeros(key.shape, jnp.float32)
        value_total = jnp.zeros(key.shape, jnp.float32)
        for h in range(len(query_parts)):
            scores = matmul(key, query_t_parts[h])
            probs = jnp.where(same, jnp.exp(scores - logs[pl.ds(h, 1), :]), 0.0)
            grad_probs = matmul(value, grad_t_parts[h])
            grad_scores = (probs * (grad_probs - deltas[h])).astype(jnp.bfloat16)
            value_total += matmul(probs.astype(jnp.bfloat16), grad_parts[h])
            key_total += matmul(grad_scores, query_parts[h])
            own = pl.ds(h * HEAD_DIM, HEAD_DIM)
            held[own, :] += matmul(key_t[h * HEAD_DIM : (h + 1) * HEAD_DIM, :], grad_scores)
        key_grad[here, :] = key_total.astype(jnp.bfloat16)
        value_grad[here, :] = value_total.astype(jnp.bfloat16)
        return carry

    lax.fori_loop(span[0], span[1], step, 0)
    query_grad_t[...] = (held[...] * factor).astype(jnp.bfloat16)


def vmem(count):
    return [pl.BlockSpec(memory_space=pltpu.SMEM)] + [
        pl.BlockSpec(memory_space=pltpu.VMEM) for _ in range(count)
    ]


def forward_attention(query_t, keys, values_t, clips):
    span, key_marks, marks = clips
    width, rows = query_t.shape
    return pl.pallas_call(
        attend_kernel,
        out_shape=(
            jax.ShapeDtypeStruct((width, rows), jnp.bfloat16),
            jax.ShapeDtypeStruct((8, rows), jnp.float32),
        ),
        in_specs=vmem(5),
        out_specs=tuple(vmem(2)[1:]),
        scratch_shapes=[pltpu.VMEM((width, rows), jnp.float32)],
        compiler_params=pltpu.CompilerParams(vmem_limit_bytes=40 * 2**20),
        name="attend",
    )(span, keys, values_t, query_t, key_marks, marks)


def backward_attention(keys, keys_t, values, query, query_t, grad, grad_t, mixed_t, logs, clips):
    span, key_marks, marks = clips
    width, rows = query_t.shape
    return pl.pallas_call(
        attend_back_kernel,
        out_shape=(
            jax.ShapeDtypeStruct((width, rows), jnp.bfloat16),
            jax.ShapeDtypeStruct(keys.shape, jnp.bfloat16),
            jax.ShapeDtypeStruct(keys.shape, jnp.bfloat16),
        ),
        in_specs=vmem(11),
        out_specs=tuple(vmem(3)[1:]),
        scratch_shapes=[pltpu.VMEM((width, rows), jnp.float32)],
        compiler_params=pltpu.CompilerParams(vmem_limit_bytes=40 * 2**20),
        name="attend_back",
    )(span, keys, keys_t, values, query, query_t, grad, grad_t, mixed_t, logs, key_marks, marks)


def clip_window(clip_here):
    marks = clip_here + 1
    key_marks = gather_window(marks)
    tiles = key_marks.reshape(-1, KEY_TILE)
    hit = jnp.any((tiles >= marks[0]) & (tiles <= marks[-1]), axis=1)
    place = jnp.arange(tiles.shape[0], dtype=jnp.int32)
    low = jnp.min(jnp.where(hit, place, tiles.shape[0]))
    high = jnp.max(jnp.where(hit, place + 1, 0))
    return (jnp.stack([low, high]), key_marks[:, None], marks[None, :])


def layer_forward(layer_in, clips, weights):
    gains, shifts, qkv_w, bias_pair, output_w, expand_w, expand_b, reduce_w = weights
    width = bias_pair.shape[-1]
    resid_in = layer_in.astype(jnp.float32)
    normed = spread_rows(norm_rows(resid_in, gains[0], shifts[0]).astype(jnp.bfloat16))
    no_bias = jnp.zeros((width,), jnp.float32)
    qkv_bias = jnp.concatenate([bias_pair[0], no_bias, bias_pair[1]])
    qkv = (matmul(normed, qkv_w) + qkv_bias).astype(jnp.bfloat16)
    query = qkv[:, :width]
    window = gather_window(qkv[:, width:])
    keys, values = window[:, :width], window[:, width:]
    query_t = query.T
    mixed_t, logs = forward_attention(query_t, keys, values.T, clips)
    resid_mid = resid_in + fold_rows(inner_rows(mixed_t, output_w)) + shifts[2]
    normed_mid = spread_rows(norm_rows(resid_mid, gains[1], shifts[1]).astype(jnp.bfloat16))
    expanded = matmul(normed_mid, expand_w) + expand_b
    activated = gelu_exact(expanded).astype(jnp.bfloat16)
    layer_out = (resid_mid + fold_rows(matmul(activated, reduce_w)) + shifts[3]).astype(
        jnp.bfloat16
    )
    saved = (
        layer_in, normed, query, query_t, keys, values, mixed_t, logs, resid_mid, normed_mid,
        expanded, activated,
    )
    return (layer_out, saved)


def layer_backward(layer_grad, saved, clips, weights, prior):
    gains, shifts, qkv_w, bias_pair, output_w, expand_w, expand_b, reduce_w = weights
    (
        layer_in, normed, query, query_t, keys, values, mixed_t, logs, resid_mid, normed_mid,
        expanded, activated,
    ) = saved
    grad_out = layer_grad.astype(jnp.float32)
    grad_all = spread_rows(layer_grad)
    grad_act = times_trans(grad_all, reduce_w)
    gelu_back = jax.vjp(gelu_exact, expanded)[1]
    grad_expanded = gelu_back(grad_act)[0].astype(jnp.bfloat16)
    grad_normed_mid = fold_rows(times_trans(grad_expanded, expand_w))
    grad_reduce = inner_rows(activated, grad_all).astype(jnp.bfloat16)
    grad_expand_bias = jnp.sum(grad_expanded, axis=0, dtype=jnp.float32)
    grad_expand = inner_rows(normed_mid, grad_expanded).astype(jnp.bfloat16)
    feed_sum = sum_half(grad_expand, grad_reduce, prior)
    mid_back = jax.vjp(norm_rows, resid_mid, gains[1], shifts[1])[1]
    grad_mid_norm, grad_gain_mid, grad_shift_mid = mid_back(grad_normed_mid)
    grad_mid = grad_out + grad_mid_norm
    grad_branch = spread_rows(grad_mid.astype(jnp.bfloat16))
    grad_mixed = times_trans(grad_branch, output_w).astype(jnp.bfloat16)
    query_grad_t, key_terms, value_terms = backward_attention(
        keys, keys.T, values, query, query_t, grad_mixed, grad_mixed.T, mixed_t, logs, clips
    )
    grad_output = matmul(mixed_t, grad_branch).astype(jnp.bfloat16)
    grad_keyval = return_window(jnp.concatenate([key_terms, value_terms], axis=1))
    grad_qkv = jnp.concatenate([query_grad_t.T, grad_keyval], axis=1)
    grad_normed = fold_rows(times_trans(grad_qkv, qkv_w))
    grad_qkv_w = inner_rows(normed, grad_qkv).astype(jnp.bfloat16)
    half = grad_qkv_w.shape[0] // 2
    half_out = grad_output.shape[0] // 2
    qkv_sum = sum_half(grad_qkv_w[:half], grad_qkv_w[half:], feed_sum)
    output_sum = sum_half(grad_output[:half_out], grad_output[half_out:], feed_sum)
    qkv_bias = jnp.sum(grad_qkv, axis=0, dtype=jnp.float32)
    in_back = jax.vjp(norm_rows, layer_in.astype(jnp.float32), gains[0], shifts[0])[1]
    grad_in_norm, grad_gain_in, grad_shift_in = in_back(grad_normed)
    input_grad = (grad_mid + grad_in_norm).astype(jnp.bfloat16)
    norms = jnp.stack(
        [
            grad_gain_in, grad_gain_mid, grad_shift_in, grad_shift_mid,
            jnp.sum(grad_mid, axis=0), jnp.sum(grad_out, axis=0),
        ]
    )
    biases = jnp.concatenate([qkv_bias, grad_expand_bias])
    return (input_grad, (feed_sum, qkv_sum, output_sum), norms, biases)


def sum_half(first, second, prior):
    core = lax.axis_index("pipe") == 0
    kept = jnp.where(core, first, second)
    got = swap_cores(jnp.where(core, second, first))
    half = kept + got
    if prior is not None:
        half, _ = lax.optimization_barrier((half, prior))
    return lax.psum(half, "seq")


def shards(
    frames,
    clip_ids,
    cotangent,
    norm_gains,
    norm_shifts,
    query_projection_weight,
    w_keyval,
    proj_bias,
    w_output,
    w_expand,
    expand_bias,
    w_reduce,
):
    core = lax.axis_index("pipe")
    low_core = core == 0
    qkv_w = jnp.concatenate([query_projection_weight[0], w_keyval[0, 0], w_keyval[0, 1]], axis=1)
    own = (
        norm_gains[0], norm_shifts[0], qkv_w, proj_bias[0], w_output[0], w_expand[0],
        expand_bias[0], w_reduce[0],
    )
    other = tuple(swap_cores(item) for item in own)
    weights = [
        tuple(jnp.where(low_core, a, b) for a, b in zip(own, other)),
        tuple(jnp.where(low_core, b, a) for a, b in zip(own, other)),
    ]
    clips = clip_window(lax.dynamic_index_in_dim(clip_ids, core, 0, keepdims=False))
    stream = lax.dynamic_index_in_dim(frames, core, 0, keepdims=False)
    outs, saved = [], []
    for number in range(2):
        stream, kept = layer_forward(stream, clips, weights[number])
        outs.append(stream)
        saved.append(kept)
    grad = lax.dynamic_index_in_dim(cotangent, core, 0, keepdims=False)
    grads, sums, norms, biases = [None] * 2, [None] * 2, [None] * 2, [None] * 2
    for number in (1, 0):
        grad, sums[number], norms[number], biases[number] = layer_backward(
            grad, saved[number], clips, weights[number], None if number == 1 else sums[1][1]
        )
        grads[number] = grad

    def both_batches(pair):
        mine = jnp.where(low_core, pair[0], pair[1])
        got = swap_cores(jnp.where(low_core, pair[1], pair[0]))
        return jnp.stack([jnp.where(low_core, mine, got), jnp.where(low_core, got, mine)])[None]

    def both_halves(place):
        mine = jnp.where(low_core, sums[0][place], sums[1][place])
        got = swap_cores(jnp.where(low_core, sums[1][place], sums[0][place]))
        return (
            jnp.where(low_core, mine, got).astype(jnp.float32),
            jnp.where(low_core, got, mine).astype(jnp.float32),
        )

    states = both_batches(outs)
    input_grads = both_batches(grads)
    grad_expand, grad_reduce = both_halves(0)
    grad_qkv = jnp.concatenate(both_halves(1), axis=0)
    grad_output = jnp.concatenate(both_halves(2), axis=0)
    norm_rows_all = jnp.pad(jnp.concatenate(norms), ((0, 4), (0, 0)))
    norm_rows_all = total_over(norm_rows_all, "tensor", 3)
    model = norm_rows_all.shape[1]
    length = biases[0].shape[0]
    bias_rows = [
        jnp.pad(item, (0, -length % model)).reshape(-1, model) for item in biases
    ]
    packed = total_over(
        jnp.concatenate([norm_rows_all[:6], bias_rows[0], norm_rows_all[6:12], bias_rows[1]]),
        "seq", 4,
    )
    half_rows = packed.shape[0] // 2
    first, second = packed[:half_rows], packed[half_rows:]
    packed = jnp.where(low_core, first, second) + swap_cores(jnp.where(low_core, second, first))
    norm_sum = packed[:6]
    bias_sum = packed[6:].reshape(-1)[:length]
    width = proj_bias.shape[-1]
    return (
        states,
        input_grads,
        norm_sum[None, :2],
        norm_sum[None, 2:],
        grad_qkv[None, :, :width],
        jnp.stack([grad_qkv[:, width : 2 * width], grad_qkv[:, 2 * width :]])[None],
        jnp.stack([bias_sum[:width], bias_sum[2 * width : 3 * width]])[None],
        grad_output[None],
        grad_expand[None],
        bias_sum[None, 3 * width :],
        grad_reduce[None],
    )


def solution(mesh):
    return jax.shard_map(
        shards,
        mesh=mesh,
        in_specs=(
            P(None, ("seq", "tensor"), None),
            P(None, "seq"),
            P(None, ("seq", "tensor"), None),
            P("pipe", None, None),
            P("pipe", None, None),
            P("pipe", None, "tensor"),
            P("pipe", None, None, "tensor"),
            P("pipe", None, "tensor"),
            P("pipe", "tensor", None),
            P("pipe", None, "tensor"),
            P("pipe", "tensor"),
            P("pipe", "tensor", None),
        ),
        out_specs=(
            P("pipe", None, ("seq", "tensor"), None),
            P("pipe", None, ("seq", "tensor"), None),
            P("pipe", None, None),
            P("pipe", None, None),
            P("pipe", None, "tensor"),
            P("pipe", None, None, "tensor"),
            P("pipe", None, "tensor"),
            P("pipe", "tensor", None),
            P("pipe", None, "tensor"),
            P("pipe", "tensor"),
            P("pipe", "tensor", None),
        ),
        check_vma=False,
    )
```

```python
import functools

import jax
import jax.numpy as jnp
from jax import lax
from jax.experimental import pallas as pl
from jax.experimental.pallas import tpu as pltpu
from jax.sharding import PartitionSpec as P

HEAD_DIM = 64
REACH = 3
KEY_TILE = 128


EPS = 1e-05
NEG = -1e30


def norm_rows(values_in, gain, shift):
    center = values_in - jnp.mean(values_in, axis=-1, keepdims=True)
    spread = jnp.mean(center * center, axis=-1, keepdims=True)
    return center * lax.rsqrt(spread + EPS) * gain + shift


def gelu_exact(values_in):
    return jax.nn.gelu(values_in, approximate=False)


def matmul(left, right):
    return jnp.dot(left, right, preferred_element_type=jnp.float32)


def inner_rows(left, right):
    return lax.dot_general(
        left, right, (((0,), (0,)), ((), ())), preferred_element_type=jnp.float32
    )


def times_trans(left, right):
    return lax.dot_general(
        left, right, (((1,), (1,)), ((), ())), preferred_element_type=jnp.float32
    )


def meet(axis):
    count = lax.axis_size(axis)
    me = lax.axis_index(axis)
    peers = [lax.rem(me + step, count) for step in range(1, count)]
    barrier = pltpu.get_barrier_semaphore()
    for peer in peers:
        pl.semaphore_signal(
            barrier, inc=1, device_id={axis: peer}, device_id_type=pl.DeviceIdType.MESH
        )
    pl.semaphore_wait(barrier, count - 1)
    return (me, peers)


def push(source, target, sent, landed, axis, peer):
    copy = pltpu.make_async_remote_copy(
        src_ref=source,
        dst_ref=target,
        send_sem=sent,
        recv_sem=landed,
        device_id={axis: peer},
        device_id_type=pl.DeviceIdType.MESH,
    )
    copy.start()
    return copy


def spread_kernel(piece, whole, sent, landed):
    me, peers = meet("tensor")
    rows = piece.shape[0]
    own = pl.ds(pl.multiple_of(me * rows, rows), rows)
    copies = [
        push(piece, whole.at[own], sent.at[k], landed.at[k], "tensor", peer)
        for k, peer in enumerate(peers)
    ]
    whole[own, :] = piece[...]
    for copy in copies:
        copy.wait()


def fold_kernel(partial, total, slots, sent, landed):
    me, peers = meet("tensor")
    rows = total.shape[0]
    copies = []
    for k, peer in enumerate(peers):
        block = partial.at[pl.ds(pl.multiple_of(peer * rows, rows), rows)]
        copies.append(push(block, slots.at[k], sent.at[k], landed.at[k], "tensor", peer))
    own = pl.ds(pl.multiple_of(me * rows, rows), rows)
    total[...] = partial[own, :].astype(jnp.float32)
    for k, copy in enumerate(copies):
        copy.wait()
        total[...] += slots[k].astype(jnp.float32)


def marks_kernel(piece, whole, sent, landed):
    me, peers = meet("seq")
    copies = [
        push(piece, whole.at[me], sent.at[k], landed.at[k], "seq", peer)
        for k, peer in enumerate(peers)
    ]
    whole[pl.ds(me, 1)] = piece[...][None]
    for copy in copies:
        copy.wait()


def total_kernel(axis, piece, total, slots, sent, landed):
    me, peers = meet(axis)
    copies = [
        push(piece, slots.at[me], sent.at[k], landed.at[k], axis, peer)
        for k, peer in enumerate(peers)
    ]
    slots[pl.ds(me, 1)] = piece[...][None]
    for copy in copies:
        copy.wait()
    result = slots[0]
    for k in range(1, slots.shape[0]):
        result = result + slots[k]
    total[...] = result


def exchange(kernel, item, out, slots, axis, number, name):
    count = lax.axis_size(axis)
    scratch = [] if slots is None else [pltpu.VMEM(slots, item.dtype)]
    return pl.pallas_call(
        kernel,
        out_shape=jax.ShapeDtypeStruct(*out),
        in_specs=[pl.BlockSpec(memory_space=pltpu.VMEM)],
        out_specs=pl.BlockSpec(memory_space=pltpu.VMEM),
        scratch_shapes=scratch
        + [pltpu.SemaphoreType.DMA((count - 1,)), pltpu.SemaphoreType.DMA((count - 1,))],
        compiler_params=pltpu.CompilerParams(
            collective_id=number, has_side_effects=True, vmem_limit_bytes=24 * 2**20
        ),
        name=name,
    )(item)


def spread_rows(piece):
    rows, width = piece.shape
    whole = (rows * lax.axis_size("tensor"), width)
    return exchange(spread_kernel, piece, (whole, piece.dtype), None, "tensor", 1, "spread")


def fold_rows(partial_sum):
    count = lax.axis_size("tensor")
    rows, width = partial_sum.shape[0] // count, partial_sum.shape[1]
    return exchange(
        fold_kernel, partial_sum.astype(jnp.bfloat16), ((rows, width), jnp.float32),
        (count - 1, rows, width), "tensor", 2, "fold",
    )


def total_over(item, axis, number):
    return exchange(
        functools.partial(total_kernel, axis), item, (item.shape, item.dtype),
        (lax.axis_size(axis), *item.shape), axis, number, "total_" + axis,
    )


def swap_cores(block):
    return lax.ppermute(block, "pipe", [(0, 1), (1, 0)])


def shifted(block, distance):
    devices = range(lax.axis_size("seq"))
    route = [(i - distance, i) for i in devices if i - distance in devices]
    return lax.ppermute(block, "seq", route)


def whole_row():
    return lax.axis_size("seq") <= 2 * REACH + 1


def gather_window(block):
    if whole_row():
        return lax.all_gather(block, "seq", axis=0, tiled=True)
    return jnp.concatenate(
        [block if o == 0 else shifted(block, o) for o in range(REACH, -REACH - 1, -1)], axis=0
    )


def return_window(terms):
    if whole_row():
        return lax.psum_scatter(terms, "seq", scatter_dimension=0, tiled=True)
    pieces = jnp.split(terms, 2 * REACH + 1, axis=0)
    total = 0.0
    for piece, offset in zip(pieces, range(REACH, -REACH - 1, -1)):
        got = piece if offset == 0 else shifted(piece, -offset)
        total = total + got.astype(jnp.float32)
    return total.astype(jnp.bfloat16)


def head_parts(matrix, axis):
    head = lax.broadcasted_iota(jnp.int32, matrix.shape, axis) // HEAD_DIM
    return [
        jnp.where(head == h, matrix, 0.0).astype(jnp.bfloat16)
        for h in range(matrix.shape[axis] // HEAD_DIM)
    ]


def attend_kernel(span, keys, values_t, query_t, key_marks, marks, mixed_t, logs, held):
    rows = query_t.shape[1]
    parts = head_parts(query_t[...].astype(jnp.float32) * HEAD_DIM**-0.5, 0)
    held[...] = jnp.zeros_like(held)
    logs[...] = jnp.zeros_like(logs)

    def step(number, carry):
        start = pl.multiple_of(number * KEY_TILE, KEY_TILE)
        key = keys[pl.ds(start, KEY_TILE), :]
        value = values_t[:, pl.ds(start, KEY_TILE)]
        same = key_marks[pl.ds(start, KEY_TILE), :] == marks[...]
        later = []
        for h, part in enumerate(parts):
            top, total = carry[h]
            scores = jnp.where(same, matmul(key, part), NEG)
            new_top = jnp.maximum(top, jnp.max(scores, axis=0, keepdims=True))
            weights = jnp.exp(scores - new_top)
            scale = jnp.exp(top - new_top)
            total = total * scale + jnp.sum(weights, axis=0, keepdims=True)
            own = pl.ds(h * HEAD_DIM, HEAD_DIM)
            held[own, :] = held[own, :] * scale + matmul(
                value[h * HEAD_DIM : (h + 1) * HEAD_DIM, :], weights.astype(jnp.bfloat16)
            )
            later.append((new_top, total))
        return tuple(later)

    first = tuple(
        (jnp.full((1, rows), NEG, jnp.float32), jnp.zeros((1, rows), jnp.float32)) for _ in parts
    )
    last = lax.fori_loop(span[0], span[1], step, first)
    for h, (top, total) in enumerate(last):
        own = pl.ds(h * HEAD_DIM, HEAD_DIM)
        mixed_t[own, :] = (held[own, :] / total).astype(jnp.bfloat16)
        logs[pl.ds(h, 1), :] = top + jnp.log(total)


def attend_back_kernel(
    span, keys, keys_t, values, query, query_t, grad, grad_t, mixed_t, logs, key_marks, marks,
    query_grad_t, key_grad, value_grad, held,
):
    factor = HEAD_DIM**-0.5
    query_parts = head_parts(query[...].astype(jnp.float32) * factor, 1)
    query_t_parts = head_parts(query_t[...].astype(jnp.float32) * factor, 0)
    grad_parts = head_parts(grad[...].astype(jnp.float32), 1)
    grad_t_parts = head_parts(grad_t[...].astype(jnp.float32), 0)
    product = grad_t[...].astype(jnp.float32) * mixed_t[...].astype(jnp.float32)
    deltas = [
        jnp.sum(product[h * HEAD_DIM : (h + 1) * HEAD_DIM, :], axis=0, keepdims=True)
        for h in range(len(query_parts))
    ]
    held[...] = jnp.zeros_like(held)
    key_grad[...] = jnp.zeros_like(key_grad)
    value_grad[...] = jnp.zeros_like(value_grad)

    def step(number, carry):
        start = pl.multiple_of(number * KEY_TILE, KEY_TILE)
        here = pl.ds(start, KEY_TILE)
        key = keys[here, :]
        key_t = keys_t[:, here]
        value = values[here, :]
        same = key_marks[here, :] == marks[...]
        key_total = jnp.zeros(key.shape, jnp.float32)
        value_total = jnp.zeros(key.shape, jnp.float32)
        for h in range(len(query_parts)):
            scores = matmul(key, query_t_parts[h])
            probs = jnp.where(same, jnp.exp(scores - logs[pl.ds(h, 1), :]), 0.0)
            grad_probs = matmul(value, grad_t_parts[h])
            grad_scores = (probs * (grad_probs - deltas[h])).astype(jnp.bfloat16)
            value_total += matmul(probs.astype(jnp.bfloat16), grad_parts[h])
            key_total += matmul(grad_scores, query_parts[h])
            own = pl.ds(h * HEAD_DIM, HEAD_DIM)
            held[own, :] += matmul(key_t[h * HEAD_DIM : (h + 1) * HEAD_DIM, :], grad_scores)
        key_grad[here, :] = key_total.astype(jnp.bfloat16)
        value_grad[here, :] = value_total.astype(jnp.bfloat16)
        return carry

    lax.fori_loop(span[0], span[1], step, 0)
    query_grad_t[...] = (held[...] * factor).astype(jnp.bfloat16)


def vmem(count):
    return [pl.BlockSpec(memory_space=pltpu.SMEM)] + [
        pl.BlockSpec(memory_space=pltpu.VMEM) for _ in range(count)
    ]


def forward_attention(query_t, keys, values_t, clips):
    span, key_marks, marks = clips
    width, rows = query_t.shape
    return pl.pallas_call(
        attend_kernel,
        out_shape=(
            jax.ShapeDtypeStruct((width, rows), jnp.bfloat16),
            jax.ShapeDtypeStruct((8, rows), jnp.float32),
        ),
        in_specs=vmem(5),
        out_specs=tuple(vmem(2)[1:]),
        scratch_shapes=[pltpu.VMEM((width, rows), jnp.float32)],
        compiler_params=pltpu.CompilerParams(vmem_limit_bytes=40 * 2**20),
        name="attend",
    )(span, keys, values_t, query_t, key_marks, marks)


def backward_attention(keys, keys_t, values, query, query_t, grad, grad_t, mixed_t, logs, clips):
    span, key_marks, marks = clips
    width, rows = query_t.shape
    return pl.pallas_call(
        attend_back_kernel,
        out_shape=(
            jax.ShapeDtypeStruct((width, rows), jnp.bfloat16),
            jax.ShapeDtypeStruct(keys.shape, jnp.bfloat16),
            jax.ShapeDtypeStruct(keys.shape, jnp.bfloat16),
        ),
        in_specs=vmem(11),
        out_specs=tuple(vmem(3)[1:]),
        scratch_shapes=[pltpu.VMEM((width, rows), jnp.float32)],
        compiler_params=pltpu.CompilerParams(vmem_limit_bytes=40 * 2**20),
        name="attend_back",
    )(span, keys, keys_t, values, query, query_t, grad, grad_t, mixed_t, logs, key_marks, marks)


def clip_window(clip_here):
    marks = clip_here + 1
    if whole_row():
        count = lax.axis_size("seq")
        key_marks = exchange(
            marks_kernel, marks.reshape(-1, KEY_TILE),
            ((count, marks.shape[0] // KEY_TILE, KEY_TILE), marks.dtype), None, "seq", 5, "marks",
        ).reshape(-1)
    else:
        key_marks = gather_window(marks)
    tiles = key_marks.reshape(-1, KEY_TILE)
    hit = jnp.any((tiles >= marks[0]) & (tiles <= marks[-1]), axis=1)
    place = jnp.arange(tiles.shape[0], dtype=jnp.int32)
    low = jnp.min(jnp.where(hit, place, tiles.shape[0]))
    high = jnp.max(jnp.where(hit, place + 1, 0))
    return (jnp.stack([low, high]), key_marks[:, None], marks[None, :])


def layer_forward(layer_in, clips, weights):
    gains, shifts, qkv_w, bias_pair, output_w, expand_w, expand_b, reduce_w = weights
    width = bias_pair.shape[-1]
    resid_in = layer_in.astype(jnp.float32)
    normed = spread_rows(norm_rows(resid_in, gains[0], shifts[0]).astype(jnp.bfloat16))
    no_bias = jnp.zeros((width,), jnp.float32)
    qkv_bias = jnp.concatenate([bias_pair[0], no_bias, bias_pair[1]])
    qkv = (matmul(normed, qkv_w) + qkv_bias).astype(jnp.bfloat16)
    query = qkv[:, :width]
    window = gather_window(qkv[:, width:])
    keys, values = window[:, :width], window[:, width:]
    query_t = query.T
    mixed_t, logs = forward_attention(query_t, keys, values.T, clips)
    resid_mid = resid_in + fold_rows(inner_rows(mixed_t, output_w)) + shifts[2]
    normed_mid = spread_rows(norm_rows(resid_mid, gains[1], shifts[1]).astype(jnp.bfloat16))
    expanded = matmul(normed_mid, expand_w) + expand_b
    activated = gelu_exact(expanded).astype(jnp.bfloat16)
    layer_out = (resid_mid + fold_rows(matmul(activated, reduce_w)) + shifts[3]).astype(
        jnp.bfloat16
    )
    saved = (
        layer_in, normed, query, query_t, keys, values, mixed_t, logs, resid_mid, normed_mid,
        expanded, activated,
    )
    return (layer_out, saved)


def layer_backward(layer_grad, saved, clips, weights, prior):
    gains, shifts, qkv_w, bias_pair, output_w, expand_w, expand_b, reduce_w = weights
    (
        layer_in, normed, query, query_t, keys, values, mixed_t, logs, resid_mid, normed_mid,
        expanded, activated,
    ) = saved
    grad_out = layer_grad.astype(jnp.float32)
    grad_all = spread_rows(layer_grad)
    grad_act = times_trans(grad_all, reduce_w)
    gelu_back = jax.vjp(gelu_exact, expanded)[1]
    grad_expanded = gelu_back(grad_act)[0].astype(jnp.bfloat16)
    grad_normed_mid = fold_rows(times_trans(grad_expanded, expand_w))
    grad_reduce = inner_rows(activated, grad_all).astype(jnp.bfloat16)
    grad_expand_bias = jnp.sum(grad_expanded, axis=0, dtype=jnp.float32)
    grad_expand = inner_rows(normed_mid, grad_expanded).astype(jnp.bfloat16)
    feed_half = add_cores(grad_expand, grad_reduce)
    if prior is None:
        early = (lax.psum(feed_half, "seq"),)
    else:
        early = sum_after((prior[1], prior[2], feed_half), prior[0])
    mid_back = jax.vjp(norm_rows, resid_mid, gains[1], shifts[1])[1]
    grad_mid_norm, grad_gain_mid, grad_shift_mid = mid_back(grad_normed_mid)
    grad_mid = grad_out + grad_mid_norm
    grad_branch = spread_rows(grad_mid.astype(jnp.bfloat16))
    grad_mixed = times_trans(grad_branch, output_w).astype(jnp.bfloat16)
    query_grad_t, key_terms, value_terms = backward_attention(
        keys, keys.T, values, query, query_t, grad_mixed, grad_mixed.T, mixed_t, logs, clips
    )
    grad_output = matmul(mixed_t, grad_branch).astype(jnp.bfloat16)
    terms = jnp.concatenate([key_terms, value_terms], axis=1)
    grad_keyval = return_window(terms)
    grad_qkv = jnp.concatenate([query_grad_t.T, grad_keyval], axis=1)
    grad_normed = fold_rows(times_trans(grad_qkv, qkv_w))
    grad_qkv_w = inner_rows(normed, grad_qkv).astype(jnp.bfloat16)
    half = grad_qkv_w.shape[0] // 2
    half_out = grad_output.shape[0] // 2
    qkv_half = add_cores(grad_qkv_w[:half], grad_qkv_w[half:])
    output_half = add_cores(grad_output[:half_out], grad_output[half_out:])
    qkv_bias = jnp.sum(grad_qkv, axis=0, dtype=jnp.float32)
    in_back = jax.vjp(norm_rows, layer_in.astype(jnp.float32), gains[0], shifts[0])[1]
    grad_in_norm, grad_gain_in, grad_shift_in = in_back(grad_normed)
    input_grad = (grad_mid + grad_in_norm).astype(jnp.bfloat16)
    norms = jnp.stack(
        [
            grad_gain_in, grad_gain_mid, grad_shift_in, grad_shift_mid,
            jnp.sum(grad_mid, axis=0), jnp.sum(grad_out, axis=0),
        ]
    )
    biases = jnp.concatenate([qkv_bias, grad_expand_bias])
    return (input_grad, (*early, qkv_half, output_half), norms, biases)


def add_cores(first, second):
    core = lax.axis_index("pipe") == 0
    kept = jnp.where(core, first, second)
    return kept + swap_cores(jnp.where(core, second, first))


def sum_after(items, prior):
    items, _ = lax.optimization_barrier((items, prior))
    return lax.psum(items, "seq")


def shards(
    frames,
    clip_ids,
    cotangent,
    norm_gains,
    norm_shifts,
    query_projection_weight,
    w_keyval,
    proj_bias,
    w_output,
    w_expand,
    expand_bias,
    w_reduce,
):
    core = lax.axis_index("pipe")
    low_core = core == 0
    qkv_w = jnp.concatenate([query_projection_weight[0], w_keyval[0, 0], w_keyval[0, 1]], axis=1)
    own = (
        norm_gains[0], norm_shifts[0], qkv_w, proj_bias[0], w_output[0], w_expand[0],
        expand_bias[0], w_reduce[0],
    )
    other = tuple(swap_cores(item) for item in own)
    weights = [
        tuple(jnp.where(low_core, a, b) for a, b in zip(own, other)),
        tuple(jnp.where(low_core, b, a) for a, b in zip(own, other)),
    ]
    clips = clip_window(lax.dynamic_index_in_dim(clip_ids, core, 0, keepdims=False))
    stream = lax.dynamic_index_in_dim(frames, core, 0, keepdims=False)
    outs, saved = [], []
    for number in range(2):
        stream, kept = layer_forward(stream, clips, weights[number])
        outs.append(stream)
        saved.append(kept)
    grad = lax.dynamic_index_in_dim(cotangent, core, 0, keepdims=False)
    grads, sums, norms, biases = [None] * 2, [None] * 2, [None] * 2, [None] * 2
    for number in (1, 0):
        grad, sums[number], norms[number], biases[number] = layer_backward(
            grad, saved[number], clips, weights[number], None if number == 1 else sums[1]
        )
        grads[number] = grad

    qkv_high, output_high, feed_low, qkv_half, output_half = sums[0]
    sums = [
        (feed_low, *sum_after((qkv_half, output_half), feed_low)),
        (sums[1][0], qkv_high, output_high),
    ]

    def both_batches(pair):
        mine = jnp.where(low_core, pair[0], pair[1])
        got = swap_cores(jnp.where(low_core, pair[1], pair[0]))
        return jnp.stack([jnp.where(low_core, mine, got), jnp.where(low_core, got, mine)])[None]

    def both_halves(place):
        mine = jnp.where(low_core, sums[0][place], sums[1][place])
        got = swap_cores(jnp.where(low_core, sums[1][place], sums[0][place]))
        return (
            jnp.where(low_core, mine, got).astype(jnp.float32),
            jnp.where(low_core, got, mine).astype(jnp.float32),
        )

    states = both_batches(outs)
    input_grads = both_batches(grads)
    grad_expand, grad_reduce = both_halves(0)
    grad_qkv = jnp.concatenate(both_halves(1), axis=0)
    grad_output = jnp.concatenate(both_halves(2), axis=0)
    norm_rows_all = jnp.pad(jnp.concatenate(norms), ((0, 4), (0, 0)))
    norm_rows_all = total_over(norm_rows_all, "tensor", 3)
    model = norm_rows_all.shape[1]
    length = biases[0].shape[0]
    bias_rows = [
        jnp.pad(item, (0, -length % model)).reshape(-1, model) for item in biases
    ]
    packed = total_over(
        jnp.concatenate([norm_rows_all[:6], bias_rows[0], norm_rows_all[6:12], bias_rows[1]]),
        "seq", 4,
    )
    half_rows = packed.shape[0] // 2
    first, second = packed[:half_rows], packed[half_rows:]
    packed = jnp.where(low_core, first, second) + swap_cores(jnp.where(low_core, second, first))
    norm_sum = packed[:6]
    bias_sum = packed[6:].reshape(-1)[:length]
    width = proj_bias.shape[-1]
    return (
        states,
        input_grads,
        norm_sum[None, :2],
        norm_sum[None, 2:],
        grad_qkv[None, :, :width],
        jnp.stack([grad_qkv[:, width : 2 * width], grad_qkv[:, 2 * width :]])[None],
        jnp.stack([bias_sum[:width], bias_sum[2 * width : 3 * width]])[None],
        grad_output[None],
        grad_expand[None],
        bias_sum[None, 3 * width :],
        grad_reduce[None],
    )


def solution(mesh):
    return jax.shard_map(
        shards,
        mesh=mesh,
        in_specs=(
            P(None, ("seq", "tensor"), None),
            P(None, "seq"),
            P(None, ("seq", "tensor"), None),
            P("pipe", None, None),
            P("pipe", None, None),
            P("pipe", None, "tensor"),
            P("pipe", None, None, "tensor"),
            P("pipe", None, "tensor"),
            P("pipe", "tensor", None),
            P("pipe", None, "tensor"),
            P("pipe", "tensor"),
            P("pipe", "tensor", None),
        ),
        out_specs=(
            P("pipe", None, ("seq", "tensor"), None),
            P("pipe", None, ("seq", "tensor"), None),
            P("pipe", None, None),
            P("pipe", None, None),
            P("pipe", None, "tensor"),
            P("pipe", None, None, "tensor"),
            P("pipe", None, "tensor"),
            P("pipe", "tensor", None),
            P("pipe", None, "tensor"),
            P("pipe", "tensor"),
            P("pipe", "tensor", None),
        ),
        check_vma=False,
    )
```
